32 devices in a mesh: seq: 8 (over z, core), tp: 4 (over y, x).
Axes of the slice: x: 2, y: 2, z: 4, core: 2. Of those that a mesh axis runs over, the one named last changes fastest.
Arguments:
- tokens: bfloat16 [2, 1536, 4096], P(None, 'seq', 'tp'), may hold values from -6 to 6
- gate_weight: bfloat16 [4096, 4096], P(None, 'tp'), may hold values from -0.09375 to 0.09375
- cand_weight: bfloat16 [4096, 4096], P(None, 'tp'), may hold values from -0.09375 to 0.09375
- forget_bias: float32 [4096], P('tp'), may hold values from -1 to 9
- readout: bfloat16 [2, 1536, 4096], P(None, 'seq', 'tp'), may hold values from -6 to 6
- advantage: int32 [2, 1536], P(None, 'seq'), may hold values from -4 to 4
Outputs:
- grad_gate: float32 [4096, 4096], P('seq', 'tp')
- grad_cand: float32 [4096, 4096], P('seq', 'tp')
- grad_tokens: bfloat16 [2, 1536, 4096], P(None, 'seq', 'tp')
The draws below stay inside these ranges and needn't reach their ends.
All inputs are finite; a program needn't handle non-finite values.
Results may differ from the reference program's by a relative error of at most 0.014.
Values may be sent and summed in bfloat16 or wider, within the bound.
A program may use at most 128 MiB of HBM per device.

```python
import jax
import jax.numpy as jnp
from jax import lax

D = 4096
H = 4096
SEQLEN = 1536


def plant(entries, stream_key, smallest, largest):
    longest = entries.shape.index(max(entries.shape))
    spots = []
    for shift in (0, 1):
        where = [jax.random.randint(jax.random.fold_in(stream_key, axis), (), 0, length) for axis, length in enumerate(entries.shape)]
        where[longest] = (where[longest] + shift) % entries.shape[longest]
        spots.append(tuple(where))
    return entries.at[spots[0]].set(smallest).at[spots[1]].set(largest)


def block_scale(own_key, shape, cuts, low, largest):
    def one(axis_at, shards_of):
        steps = jax.random.uniform(jax.random.fold_in(jax.random.fold_in(own_key, 6), axis_at), (shards_of,), jnp.float32, low / len(cuts), largest / len(cuts))
        return jnp.repeat(jnp.exp(steps), shape[axis_at] // shards_of).reshape((-1,) + (1,) * (len(shape) - axis_at - 1))

    level = one(*cuts[0])
    for cut in cuts[1:]:
        level = level * one(*cut)
    return level


def normal_values(stream_key, extent, deviation, most, pieces=(), held_as=jnp.bfloat16):
    values = jax.random.normal(stream_key, extent, jnp.float32) * deviation
    if len(pieces) > 0:
        values = block_scale(stream_key, extent, pieces, -0.22, 0.18) * values
    return jnp.clip(values, min=-most, max=most).astype(held_as)


def setup_inputs(seed: int = 0) -> dict:
    keys = jax.random.split(jax.random.key(seed), 7)
    tokens = normal_values(keys[0], (2, SEQLEN, D), 1.0, 6.0, ((1, 8), (2, 4)))
    gate_weight = normal_values(keys[1], (D, H), D ** -0.5, 0.09375, ((1, 4),))
    cand_weight = normal_values(keys[2], (D, H), D ** -0.5, 0.09375, ((1, 4),))
    forget_bias = jnp.clip(-1.0 + 10.0 * jax.random.uniform(keys[3], (H,), jnp.float32) ** block_scale(keys[3], (H,), ((0, 4),), -0.2, 0.2), -1.0, 9.0)
    readout = normal_values(keys[4], (2, SEQLEN, H), 1.0, 6.0, ((1, 8), (2, 4)))
    advantage = plant(jax.random.randint(keys[5], (2, SEQLEN), -4, 5), jax.random.fold_in(keys[5], 1), -4, 4).astype(jnp.int32)
    return {"tokens": tokens, "gate_weight": gate_weight, "cand_weight": cand_weight, "forget_bias": forget_bias, "readout": readout, "advantage": advantage}


def reference(tokens, gate_weight, cand_weight, forget_bias, readout, advantage):
    flat = tokens.reshape(-1, D)
    pre = jnp.dot(flat, gate_weight, preferred_element_type=jnp.float32).reshape(2, SEQLEN, H)
    cand = jnp.dot(flat, cand_weight, preferred_element_type=jnp.float32).reshape(2, SEQLEN, H)
    keep = jax.nn.sigmoid(pre + forget_bias.astype(jnp.float32))

    def forward(carry, inputs):
        kept, fresh = inputs
        carry = kept * carry + (1.0 - kept) * fresh
        return carry, carry

    start = jnp.zeros((2, H), jnp.float32)
    _, states = lax.scan(forward, start, (jnp.moveaxis(keep, 1, 0), jnp.moveaxis(cand, 1, 0)))
    state = jnp.moveaxis(states, 0, 1)
    prev = jnp.concatenate([jnp.zeros((2, 1, H), jnp.float32), state[:, :-1]], axis=1)
    score = (advantage.astype(jnp.float32) * 0.25)[:, :, None] * readout.astype(jnp.float32)
    coef = jnp.concatenate([keep[:, 1:], jnp.ones((2, 1, H), jnp.float32)], axis=1)

    def backward(carry, inputs):
        factor, term = inputs
        carry = term + factor * carry
        return carry, carry

    _, adjoints = lax.scan(backward, start, (jnp.moveaxis(coef, 1, 0), jnp.moveaxis(score, 1, 0)), reverse=True)
    adjoint = jnp.moveaxis(adjoints, 0, 1)
    dpre = (adjoint * (prev - cand) * keep * (1.0 - keep)).astype(jnp.bfloat16).reshape(-1, H)
    dcand = (adjoint * (1.0 - keep)).astype(jnp.bfloat16).reshape(-1, H)
    grad_gate = jnp.dot(flat.T, dpre, preferred_element_type=jnp.float32)
    grad_cand = jnp.dot(flat.T, dcand, preferred_element_type=jnp.float32)
    inputs_grad = jnp.dot(dpre, gate_weight.T, preferred_element_type=jnp.float32) + jnp.dot(dcand, cand_weight.T, preferred_element_type=jnp.float32)
    grad_tokens = inputs_grad.astype(jnp.bfloat16).reshape(2, SEQLEN, D)
    return grad_gate, grad_cand, grad_tokens
```

```python
import functools

import jax
import jax.numpy as jnp
from jax import lax
from jax.experimental import pallas as pl
from jax.experimental.pallas import tpu as pltpu
from jax.sharding import PartitionSpec as P

SEGS = 8
LANE = 128


def project_kernel(flat, gate, cand_w, bias, read, scale, keep_out, cand_out, seg_out, span_out, score):
    count = flat.shape[0] // 2
    steps = count // SEGS
    lanes = gate.shape[1] // LANE
    pre = jnp.dot(flat[...], gate[...], preferred_element_type=jnp.float32)
    keep = jax.nn.sigmoid(pre + bias[...])
    cand = jnp.dot(flat[...], cand_w[...], preferred_element_type=jnp.float32)
    value = scale[...] * read[...].astype(jnp.float32)
    for l in range(lanes):
        keep_out[l] = keep[:, l * LANE : (l + 1) * LANE]
        cand_out[l] = cand[:, l * LANE : (l + 1) * LANE]
        score[l] = value[:, l * LANE : (l + 1) * LANE]
    span_out[...] = jnp.zeros_like(span_out)
    zero = jnp.zeros((SEGS, LANE), jnp.float32)
    pairs = [(b, l) for b in range(2) for l in range(lanes)]
    muls = [zero + 1.0 for _ in pairs]
    adds = [zero for _ in pairs]
    gs = [zero for _ in pairs]
    for i in range(steps):
        for p, (b, l) in enumerate(pairs):
            rows = pl.ds(b * count + i, SEGS, stride=steps)
            k = keep_out[l, rows, :]
            c = cand_out[l, rows, :]
            muls[p] = muls[p] * k
            adds[p] = k * adds[p] + (1.0 - k) * c
            rows = pl.ds(b * count + steps - 1 - i, SEGS, stride=steps)
            gs[p] = keep_out[l, rows, :] * (score[l, rows, :] + gs[p])
    for p, (b, l) in enumerate(pairs):
        at = slice(l * LANE, (l + 1) * LANE)
        mul, add, g = muls[p], adds[p], gs[p]
        seg_out[0, b, :, at] = mul
        seg_out[1, b, :, at] = add
        seg_out[2, b, :, at] = g
        m = mul[0:1]
        a = add[0:1]
        r = g[SEGS - 1 :]
        for j in range(1, SEGS):
            m = m * mul[j : j + 1]
            a = mul[j : j + 1] * a + add[j : j + 1]
            e = SEGS - 1 - j
            r = mul[e : e + 1] * r + g[e : e + 1]
        span_out[b : b + 1, at] = m
        span_out[2 + b : 3 + b, at] = a
        span_out[4 + b : 5 + b, at] = r


def delta_kernel(devices, where, spans, seg, keep, cand, read, scale, dpre_out, dcand_out, score, dp, dc):
    lanes, rows_all, _ = keep.shape
    count = rows_all // 2
    steps = count // SEGS
    me = where[0]
    value = scale[...] * read[...].astype(jnp.float32)
    pairs = [(b, l) for b in range(2) for l in range(lanes)]
    states, tails = [], []
    for l in range(lanes):
        score[l] = value[:, l * LANE : (l + 1) * LANE]
    for b, l in pairs:
        at = slice(l * LANE, (l + 1) * LANE)
        a = jnp.zeros((1, LANE), jnp.float32)
        r = a
        for d in range(devices):
            e = devices - 1 - d
            a = jnp.where(d < me, spans[d, b : b + 1, at] * a + spans[d, 2 + b : 3 + b, at], a)
            r = jnp.where(e > me, spans[e, b : b + 1, at] * r + spans[e, 4 + b : 5 + b, at], r)
        mul, add, g = seg[0, b, :, at], seg[1, b, :, at], seg[2, b, :, at]
        starts, ends = [a], [r]
        for j in range(SEGS - 1):
            a = mul[j : j + 1] * a + add[j : j + 1]
            starts.append(a)
            e = SEGS - 1 - j
            r = mul[e : e + 1] * r + g[e : e + 1]
            ends.append(r)
        states.append(jnp.concatenate(starts, axis=0))
        tails.append(jnp.concatenate(ends[::-1], axis=0))
    for i in range(steps):
        for p, (b, l) in enumerate(pairs):
            rows = pl.ds(b * count + i, SEGS, stride=steps)
            k = keep[l, rows, :]
            c = cand[l, rows, :]
            dp[l, rows, :] = (states[p] - c) * k * (1.0 - k)
            states[p] = k * states[p] + (1.0 - k) * c
    for i in range(steps):
        for p, (b, l) in enumerate(pairs):
            rows = pl.ds(b * count + steps - 1 - i, SEGS, stride=steps)
            k = keep[l, rows, :]
            adj = score[l, rows, :] + tails[p]
            dp[l, rows, :] = adj * dp[l, rows, :]
            dc[l, rows, :] = adj * (1.0 - k)
            tails[p] = k * adj
    for l in range(lanes):
        at = slice(l * LANE, (l + 1) * LANE)
        dpre_out[:, at] = dp[l].astype(jnp.bfloat16)
        dcand_out[:, at] = dc[l].astype(jnp.bfloat16)


def shards(tokens, gate_weight, cand_weight, forget_bias, readout, advantage):
    devices = lax.axis_size("seq")
    groups = lax.axis_size("tp")
    whole = lax.all_gather(tokens, "tp", axis=2, tiled=True)
    count = whole.shape[1]
    depth = whole.shape[2]
    rows = 2 * count
    width = gate_weight.shape[1]
    flat = whole.reshape(rows, depth)
    part = rows // groups
    mine = lax.dynamic_slice_in_dim(flat, lax.axis_index("tp") * part, part, 0)
    mine = lax.all_to_all(mine, "seq", split_axis=1, concat_axis=0, tiled=True)
    cols = lax.all_gather(mine, "tp", axis=0, tiled=False)
    cols = cols.reshape(groups, devices, part, depth // devices)
    cols = jnp.transpose(cols, (1, 0, 2, 3)).reshape(devices * rows, depth // devices)

    scale = (advantage.astype(jnp.float32) * 0.25).reshape(rows, 1)
    read = readout.reshape(rows, width)
    tile = 256 if width % 256 == 0 else width
    f32 = jnp.float32
    col = pl.BlockSpec((rows, tile), lambda i: (0, i))
    lane = pl.BlockSpec((tile // LANE, rows, LANE), lambda i: (i, 0, 0))
    full_scale = pl.BlockSpec((rows, 1), lambda i: (0, 0))
    seg_spec = pl.BlockSpec((3, 2, SEGS, tile), lambda i: (0, 0, 0, i))
    keep, cand, seg, span = pl.pallas_call(
        project_kernel,
        grid=(width // tile,),
        in_specs=[
            pl.BlockSpec((rows, depth), lambda i: (0, 0)),
            pl.BlockSpec((depth, tile), lambda i: (0, i)),
            pl.BlockSpec((depth, tile), lambda i: (0, i)),
            pl.BlockSpec((1, tile), lambda i: (0, i)),
            col,
            full_scale,
        ],
        out_specs=[lane, lane, seg_spec, pl.BlockSpec((8, tile), lambda i: (0, i))],
        out_shape=[
            jax.ShapeDtypeStruct((width // LANE, rows, LANE), f32),
            jax.ShapeDtypeStruct((width // LANE, rows, LANE), f32),
            jax.ShapeDtypeStruct((3, 2, SEGS, width), f32),
            jax.ShapeDtypeStruct((8, width), f32),
        ],
        scratch_shapes=[pltpu.VMEM((tile // LANE, rows, LANE), f32)],
        compiler_params=pltpu.CompilerParams(vmem_limit_bytes=48 << 20),
        cost_estimate=pl.CostEstimate(flops=4 * rows * depth * width, bytes_accessed=4 * depth * width, transcendentals=rows * width),
    )(flat, gate_weight, cand_weight, forget_bias.reshape(1, width), read, scale)
    spans = lax.all_gather(span, "seq", axis=0, tiled=False)
    where = lax.axis_index("seq").astype(jnp.int32).reshape(1)
    dpre, dcand = pl.pallas_call(
        functools.partial(delta_kernel, devices),
        grid=(width // tile,),
        in_specs=[
            pl.BlockSpec(memory_space=pltpu.SMEM),
            pl.BlockSpec((devices, 8, tile), lambda i: (0, 0, i)),
            seg_spec,
            lane,
            lane,
            col,
            full_scale,
        ],
        out_specs=[col, col],
        out_shape=[jax.ShapeDtypeStruct((rows, width), jnp.bfloat16)] * 2,
        scratch_shapes=[pltpu.VMEM((tile // LANE, rows, LANE), f32)] * 3,
        compiler_params=pltpu.CompilerParams(vmem_limit_bytes=48 << 20),
    )(where, spans, seg, keep, cand, read, scale)

    contract0 = (((0,), (0,)), ((), ()))
    contract1 = (((1,), (1,)), ((), ()))
    all_dpre = lax.all_gather(dpre, "seq", axis=0, tiled=True)
    all_dcand = lax.all_gather(dcand, "seq", axis=0, tiled=True)
    term = lax.dot_general(dpre, gate_weight, contract1, preferred_element_type=f32)
    term = term + lax.dot_general(dcand, cand_weight, contract1, preferred_element_type=f32)
    term = term.astype(jnp.bfloat16).reshape(2, count, depth)
    grad_tokens = lax.psum_scatter(term, "tp", scatter_dimension=2, tiled=True)
    grad_gate = lax.dot_general(cols, all_dpre, contract0, preferred_element_type=f32)
    grad_cand = lax.dot_general(cols, all_dcand, contract0, preferred_element_type=f32)
    return (grad_gate, grad_cand, grad_tokens)


def solution(mesh):
    in_specs = (
        P(None, "seq", "tp"),
        P(None, "tp"),
        P(None, "tp"),
        P("tp"),
        P(None, "seq", "tp"),
        P(None, "seq"),
    )
    out_specs = (P("seq", "tp"), P("seq", "tp"), P(None, "seq", "tp"))
    return jax.shard_map(shards, mesh=mesh, in_specs=in_specs, out_specs=out_specs, check_vma=False)
```

```python
import functools

import jax
import jax.numpy as jnp
from jax import lax
from jax.experimental import pallas as pl
from jax.experimental.pallas import tpu as pltpu
from jax.sharding import PartitionSpec as P

SEGS = 8
LANE = 128


def project_kernel(flat, gate, cand_w, bias, read, scale, keep_out, cand_out, seg_out, span_out, score):
    count = flat.shape[0] // 2
    steps = count // SEGS
    lanes = gate.shape[1] // LANE
    pre = jnp.dot(flat[...], gate[...], preferred_element_type=jnp.float32)
    keep = jax.nn.sigmoid(pre + bias[...])
    cand = jnp.dot(flat[...], cand_w[...], preferred_element_type=jnp.float32)
    value = scale[...] * read[...].astype(jnp.float32)
    for l in range(lanes):
        keep_out[l] = keep[:, l * LANE : (l + 1) * LANE]
        cand_out[l] = cand[:, l * LANE : (l + 1) * LANE]
        score[l] = value[:, l * LANE : (l + 1) * LANE]
    span_out[...] = jnp.zeros_like(span_out)
    zero = jnp.zeros((SEGS, LANE), jnp.float32)
    pairs = [(b, l) for b in range(2) for l in range(lanes)]
    muls = [zero + 1.0 for _ in pairs]
    adds = [zero for _ in pairs]
    gs = [zero for _ in pairs]
    for i in range(steps):
        for p, (b, l) in enumerate(pairs):
            rows = pl.ds(b * count + i, SEGS, stride=steps)
            k = keep_out[l, rows, :]
            c = cand_out[l, rows, :]
            muls[p] = muls[p] * k
            adds[p] = k * adds[p] + (1.0 - k) * c
            rows = pl.ds(b * count + steps - 1 - i, SEGS, stride=steps)
            gs[p] = keep_out[l, rows, :] * (score[l, rows, :] + gs[p])
    for p, (b, l) in enumerate(pairs):
        at = slice(l * LANE, (l + 1) * LANE)
        mul, add, g = muls[p], adds[p], gs[p]
        seg_out[0, b, :, at] = mul
        seg_out[1, b, :, at] = add
        seg_out[2, b, :, at] = g
        m = mul[0:1]
        a = add[0:1]
        r = g[SEGS - 1 :]
        for j in range(1, SEGS):
            m = m * mul[j : j + 1]
            a = mul[j : j + 1] * a + add[j : j + 1]
            e = SEGS - 1 - j
            r = mul[e : e + 1] * r + g[e : e + 1]
        span_out[b : b + 1, at] = m
        span_out[2 + b : 3 + b, at] = a
        span_out[4 + b : 5 + b, at] = r


def delta_kernel(devices, where, spans, seg, keep, cand, read, scale, delta_out, score, dp, dc):
    lanes, rows_all, _ = keep.shape
    count = rows_all // 2
    steps = count // SEGS
    me = where[0]
    value = scale[...] * read[...].astype(jnp.float32)
    pairs = [(b, l) for b in range(2) for l in range(lanes)]
    states, tails = [], []
    for l in range(lanes):
        score[l] = value[:, l * LANE : (l + 1) * LANE]
    for b, l in pairs:
        at = slice(l * LANE, (l + 1) * LANE)
        a = jnp.zeros((1, LANE), jnp.float32)
        r = a
        for d in range(devices):
            e = devices - 1 - d
            a = jnp.where(d < me, spans[d, b : b + 1, at] * a + spans[d, 2 + b : 3 + b, at], a)
            r = jnp.where(e > me, spans[e, b : b + 1, at] * r + spans[e, 4 + b : 5 + b, at], r)
        mul, add, g = seg[0, b, :, at], seg[1, b, :, at], seg[2, b, :, at]
        starts, ends = [a], [r]
        for j in range(SEGS - 1):
            a = mul[j : j + 1] * a + add[j : j + 1]
            starts.append(a)
            e = SEGS - 1 - j
            r = mul[e : e + 1] * r + g[e : e + 1]
            ends.append(r)
        states.append(jnp.concatenate(starts, axis=0))
        tails.append(jnp.concatenate(ends[::-1], axis=0))
    for i in range(steps):
        for p, (b, l) in enumerate(pairs):
            rows = pl.ds(b * count + i, SEGS, stride=steps)
            k = keep[l, rows, :]
            c = cand[l, rows, :]
            dp[l, rows, :] = (states[p] - c) * k * (1.0 - k)
            states[p] = k * states[p] + (1.0 - k) * c
    for i in range(steps):
        for p, (b, l) in enumerate(pairs):
            rows = pl.ds(b * count + steps - 1 - i, SEGS, stride=steps)
            k = keep[l, rows, :]
            adj = score[l, rows, :] + tails[p]
            dp[l, rows, :] = adj * dp[l, rows, :]
            dc[l, rows, :] = adj * (1.0 - k)
            tails[p] = k * adj
    for l in range(lanes):
        at = slice(l * LANE, (l + 1) * LANE)
        delta_out[0, :, at] = dp[l].astype(jnp.bfloat16)
        delta_out[1, :, at] = dc[l].astype(jnp.bfloat16)


def exchange_kernel(chips, groups, delta, cols, gate_hbm, cand_hbm, gate_out, cand_out, tok_out,
                    slots, weights, partial, landed, w_sem, own_sem, send_sem, pass_sem, recv_sem, part_send, part_recv):
    seq = lax.axis_index("seq")
    tp = lax.axis_index("tp")
    chip = lax.div(seq, 2)
    core = lax.rem(seq, 2)
    sibling = chip * 2 + 1 - core
    block = weights.shape[2]
    mesh_id = pl.DeviceIdType.MESH

    barrier = pltpu.get_barrier_semaphore()
    for d in range(1, chips):
        other = lax.rem(chip + d, chips) * 2 + core
        pl.semaphore_signal(barrier, inc=1, device_id=(other, tp), device_id_type=mesh_id)
    pl.semaphore_signal(barrier, inc=1, device_id=(sibling, tp), device_id_type=mesh_id)
    for d in range(1, groups):
        pl.semaphore_signal(barrier, inc=1, device_id=(seq, lax.rem(tp + d, groups)), device_id_type=mesh_id)

    def fetch(p, buf):
        rows = pl.ds(pl.multiple_of(lax.rem(tp + p, groups) * block, 128), block)
        return [
            pltpu.make_async_copy(w.at[rows, :], weights.at[buf, k], w_sem.at[buf, k])
            for k, w in enumerate((gate_hbm, cand_hbm))
        ]

    for copy in fetch(1 % groups, 0):
        copy.start()
    pl.semaphore_wait(barrier, chips - 1 + 1 + groups - 1)

    def send(kind, d):
        other = lax.rem(chip + d, chips) * 2 + core
        return pltpu.make_async_remote_copy(
            src_ref=delta.at[kind], dst_ref=slots.at[seq, kind], send_sem=send_sem.at[kind, d],
            recv_sem=recv_sem.at[seq, kind], device_id=(other, tp), device_id_type=mesh_id)

    def receive(kind, origin):
        return pltpu.make_async_remote_copy(
            src_ref=delta.at[kind], dst_ref=slots.at[origin, kind], send_sem=send_sem.at[kind, 0],
            recv_sem=recv_sem.at[origin, kind], device_id=(sibling, tp), device_id_type=mesh_id)

    def hand(kind, d):
        origin = lax.rem(chip + d, chips) * 2 + core
        return pltpu.make_async_remote_copy(
            src_ref=slots.at[origin, kind], dst_ref=slots.at[origin, kind], send_sem=pass_sem.at[kind, d],
            recv_sem=recv_sem.at[origin, kind], device_id=(sibling, tp), device_id_type=mesh_id)

    def own(kind):
        return pltpu.make_async_copy(delta.at[kind], slots.at[seq, kind], own_sem.at[kind])

    for kind in range(2):
        own(kind).start()
        for d in range(1, chips):
            send(kind, d).start()
    for kind in range(2):
        own(kind).wait()
        hand(kind, 0).start()

    nt = (((1,), (1,)), ((), ()))
    tn = (((0,), (0,)), ((), ()))
    f32 = jnp.float32

    def share(p, buf):
        for copy in fetch(p, buf):
            copy.wait()
        term = lax.dot_general(delta[0], weights[buf, 0], nt, preferred_element_type=f32)
        return term + lax.dot_general(delta[1], weights[buf, 1], nt, preferred_element_type=f32)

    def give(p):
        return pltpu.make_async_remote_copy(
            src_ref=partial.at[p - 1], dst_ref=landed.at[p - 1], send_sem=part_send.at[p - 1],
            recv_sem=part_recv.at[p - 1], device_id=(seq, lax.rem(tp + p, groups)), device_id_type=mesh_id)

    for p in range(1, groups):
        for copy in fetch((p + 1) % groups, p % 2):
            copy.start()
        partial[p - 1] = share(p, (p - 1) % 2).astype(jnp.bfloat16)
        give(p).start()
    mine = share(0, (groups - 1) % 2)
    for p in range(1, groups):
        give(p).wait()
        mine = mine + landed[p - 1].astype(f32)
    tok_out[...] = mine.astype(jnp.bfloat16)

    gate_out[...] = jnp.zeros_like(gate_out)
    cand_out[...] = jnp.zeros_like(cand_out)
    for kind, out in enumerate((gate_out, cand_out)):

        def step(d, carry):
            at = lax.rem(chip + d, chips) * 2
            lane = at + core

            @pl.when(d > 0)
            def _():
                receive(kind, lane).wait_recv()
                hand(kind, d).start()

            out[...] += lax.dot_general(cols[lane], slots[lane, kind], tn, preferred_element_type=f32)
            other = at + 1 - core
            receive(kind, other).wait_recv()
            out[...] += lax.dot_general(cols[other], slots[other, kind], tn, preferred_element_type=f32)
            return carry

        lax.fori_loop(0, chips, step, 0)
    for kind in range(2):
        for d in range(chips):
            if d > 0:
                send(kind, d).wait_send()
            hand(kind, d).wait_send()


def shards(tokens, gate_weight, cand_weight, forget_bias, readout, advantage):
    devices = lax.axis_size("seq")
    groups = lax.axis_size("tp")
    whole = lax.all_gather(tokens, "tp", axis=2, tiled=True)
    count = whole.shape[1]
    depth = whole.shape[2]
    rows = 2 * count
    width = gate_weight.shape[1]
    flat = whole.reshape(rows, depth)
    part = rows // groups
    mine = lax.dynamic_slice_in_dim(flat, lax.axis_index("tp") * part, part, 0)
    mine = lax.all_to_all(mine, "seq", split_axis=1, concat_axis=0, tiled=True)
    cols = lax.all_gather(mine, "tp", axis=0, tiled=False)
    cols = cols.reshape(groups, devices, part, depth // devices)
    cols = jnp.transpose(cols, (1, 0, 2, 3)).reshape(devices, rows, depth // devices)

    scale = (advantage.astype(jnp.float32) * 0.25).reshape(rows, 1)
    read = readout.reshape(rows, width)
    tile = 256 if width % 256 == 0 else width
    f32 = jnp.float32
    col = pl.BlockSpec((rows, tile), lambda i: (0, i))
    lane = pl.BlockSpec((tile // LANE, rows, LANE), lambda i: (i, 0, 0))
    full_scale = pl.BlockSpec((rows, 1), lambda i: (0, 0))
    seg_spec = pl.BlockSpec((3, 2, SEGS, tile), lambda i: (0, 0, 0, i))
    keep, cand, seg, span = pl.pallas_call(
        project_kernel,
        grid=(width // tile,),
        in_specs=[
            pl.BlockSpec((rows, depth), lambda i: (0, 0)),
            pl.BlockSpec((depth, tile), lambda i: (0, i)),
            pl.BlockSpec((depth, tile), lambda i: (0, i)),
            pl.BlockSpec((1, tile), lambda i: (0, i)),
            col,
            full_scale,
        ],
        out_specs=[lane, lane, seg_spec, pl.BlockSpec((8, tile), lambda i: (0, i))],
        out_shape=[
            jax.ShapeDtypeStruct((width // LANE, rows, LANE), f32),
            jax.ShapeDtypeStruct((width // LANE, rows, LANE), f32),
            jax.ShapeDtypeStruct((3, 2, SEGS, width), f32),
            jax.ShapeDtypeStruct((8, width), f32),
        ],
        scratch_shapes=[pltpu.VMEM((tile // LANE, rows, LANE), f32)],
        compiler_params=pltpu.CompilerParams(vmem_limit_bytes=48 << 20),
        cost_estimate=pl.CostEstimate(flops=4 * rows * depth * width, bytes_accessed=4 * depth * width, transcendentals=rows * width),
    )(flat, gate_weight, cand_weight, forget_bias.reshape(1, width), read, scale)
    spans = lax.all_gather(span, "seq", axis=0, tiled=False)
    where = lax.axis_index("seq").astype(jnp.int32).reshape(1)
    delta = pl.pallas_call(
        functools.partial(delta_kernel, devices),
        grid=(width // tile,),
        in_specs=[
            pl.BlockSpec(memory_space=pltpu.SMEM),
            pl.BlockSpec((devices, 8, tile), lambda i: (0, 0, i)),
            seg_spec,
            lane,
            lane,
            col,
            full_scale,
        ],
        out_specs=pl.BlockSpec((2, rows, tile), lambda i: (0, 0, i)),
        out_shape=jax.ShapeDtypeStruct((2, rows, width), jnp.bfloat16),
        scratch_shapes=[pltpu.VMEM((tile // LANE, rows, LANE), f32)] * 3,
        compiler_params=pltpu.CompilerParams(vmem_limit_bytes=48 << 20),
    )(where, spans, seg, keep, cand, read, scale)

    chips = devices // 2
    block = depth // groups
    bf16 = jnp.bfloat16
    dma = pltpu.SemaphoreType.DMA
    vmem = pl.BlockSpec(memory_space=pltpu.VMEM)
    grad_gate, grad_cand, grad_tokens = pl.pallas_call(
        functools.partial(exchange_kernel, chips, groups),
        in_specs=[vmem, vmem, pl.BlockSpec(memory_space=pl.ANY), pl.BlockSpec(memory_space=pl.ANY)],
        out_specs=[vmem, vmem, vmem],
        out_shape=[
            jax.ShapeDtypeStruct((depth // devices, width), f32),
            jax.ShapeDtypeStruct((depth // devices, width), f32),
            jax.ShapeDtypeStruct((rows, block), bf16),
        ],
        scratch_shapes=[
            pltpu.VMEM((devices, 2, rows, width), bf16),
            pltpu.VMEM((2, 2, block, width), bf16),
            pltpu.VMEM((groups - 1, rows, block), bf16),
            pltpu.VMEM((groups - 1, rows, block), bf16),
            dma((2, 2)),
            dma((2,)),
            dma((2, chips)),
            dma((2, chips)),
            dma((devices, 2)),
            dma((groups - 1,)),
            dma((groups - 1,)),
        ],
        compiler_params=pltpu.CompilerParams(collective_id=1, has_side_effects=True, vmem_limit_bytes=56 << 20),
        cost_estimate=pl.CostEstimate(flops=12 * rows * depth * width, bytes_accessed=24 << 20, transcendentals=0),
    )(delta, cols, gate_weight, cand_weight)
    return (grad_gate, grad_cand, grad_tokens.reshape(2, count, block))


def solution(mesh):
    in_specs = (
        P(None, "seq", "tp"),
        P(None, "tp"),
        P(None, "tp"),
        P("tp"),
        P(None, "seq", "tp"),
        P(None, "seq"),
    )
    out_specs = (P("seq", "tp"), P("seq", "tp"), P(None, "seq", "tp"))
    return jax.shard_map(shards, mesh=mesh, in_specs=in_specs, out_specs=out_specs, check_vma=False)
```

```python
import functools

import jax
import jax.numpy as jnp
from jax import lax
from jax.experimental import pallas as pl
from jax.experimental.pallas import tpu as pltpu
from jax.sharding import PartitionSpec as P

SEGS = 8
LANE = 128


def project_kernel(flat, gate, cand_w, bias, read, scale, keep_out, cand_out, seg_out, span_out, score):
    count = flat.shape[0] // 2
    steps = count // SEGS
    lanes = gate.shape[1] // LANE
    pre = jnp.dot(flat[...], gate[...], preferred_element_type=jnp.float32)
    keep = jax.nn.sigmoid(pre + bias[...])
    cand = jnp.dot(flat[...], cand_w[...], preferred_element_type=jnp.float32)
    value = scale[...] * read[...].astype(jnp.float32)
    for l in range(lanes):
        keep_out[l] = keep[:, l * LANE : (l + 1) * LANE]
        cand_out[l] = cand[:, l * LANE : (l + 1) * LANE]
        score[l] = value[:, l * LANE : (l + 1) * LANE]
    span_out[...] = jnp.zeros_like(span_out)
    zero = jnp.zeros((SEGS, LANE), jnp.float32)
    pairs = [(b, l) for b in range(2) for l in range(lanes)]
    muls = [zero + 1.0 for _ in pairs]
    adds = [zero for _ in pairs]
    gs = [zero for _ in pairs]
    for i in range(steps):
        for p, (b, l) in enumerate(pairs):
            rows = pl.ds(b * count + i, SEGS, stride=steps)
            k = keep_out[l, rows, :]
            c = cand_out[l, rows, :]
            muls[p] = muls[p] * k
            adds[p] = k * adds[p] + (1.0 - k) * c
            rows = pl.ds(b * count + steps - 1 - i, SEGS, stride=steps)
            gs[p] = keep_out[l, rows, :] * (score[l, rows, :] + gs[p])
    for p, (b, l) in enumerate(pairs):
        at = slice(l * LANE, (l + 1) * LANE)
        mul, add, g = muls[p], adds[p], gs[p]
        seg_out[0, b, :, at] = mul
        seg_out[1, b, :, at] = add
        seg_out[2, b, :, at] = g
        m = mul[0:1]
        a = add[0:1]
        r = g[SEGS - 1 :]
        for j in range(1, SEGS):
            m = m * mul[j : j + 1]
            a = mul[j : j + 1] * a + add[j : j + 1]
            e = SEGS - 1 - j
            r = mul[e : e + 1] * r + g[e : e + 1]
        span_out[b : b + 1, at] = m
        span_out[2 + b : 3 + b, at] = a
        span_out[4 + b : 5 + b, at] = r


def delta_kernel(devices, where, spans, seg, keep, cand, read, scale, delta_out, score, dp, dc):
    lanes, rows_all, _ = keep.shape
    count = rows_all // 2
    steps = count // SEGS
    me = where[0]
    value = scale[...] * read[...].astype(jnp.float32)
    pairs = [(b, l) for b in range(2) for l in range(lanes)]
    states, tails = [], []
    for l in range(lanes):
        score[l] = value[:, l * LANE : (l + 1) * LANE]
    for b, l in pairs:
        at = slice(l * LANE, (l + 1) * LANE)
        a = jnp.zeros((1, LANE), jnp.float32)
        r = a
        for d in range(devices):
            e = devices - 1 - d
            a = jnp.where(d < me, spans[d, b : b + 1, at] * a + spans[d, 2 + b : 3 + b, at], a)
            r = jnp.where(e > me, spans[e, b : b + 1, at] * r + spans[e, 4 + b : 5 + b, at], r)
        mul, add, g = seg[0, b, :, at], seg[1, b, :, at], seg[2, b, :, at]
        starts, ends = [a], [r]
        for j in range(SEGS - 1):
            a = mul[j : j + 1] * a + add[j : j + 1]
            starts.append(a)
            e = SEGS - 1 - j
            r = mul[e : e + 1] * r + g[e : e + 1]
            ends.append(r)
        states.append(jnp.concatenate(starts, axis=0))
        tails.append(jnp.concatenate(ends[::-1], axis=0))
    for i in range(steps):
        for p, (b, l) in enumerate(pairs):
            rows = pl.ds(b * count + i, SEGS, stride=steps)
            k = keep[l, rows, :]
            c = cand[l, rows, :]
            dp[l, rows, :] = (states[p] - c) * k * (1.0 - k)
            states[p] = k * states[p] + (1.0 - k) * c
    for i in range(steps):
        for p, (b, l) in enumerate(pairs):
            rows = pl.ds(b * count + steps - 1 - i, SEGS, stride=steps)
            k = keep[l, rows, :]
            adj = score[l, rows, :] + tails[p]
            dp[l, rows, :] = adj * dp[l, rows, :]
            dc[l, rows, :] = adj * (1.0 - k)
            tails[p] = k * adj
    for l in range(lanes):
        at = slice(l * LANE, (l + 1) * LANE)
        delta_out[0, :, at] = dp[l].astype(jnp.bfloat16)
        delta_out[1, :, at] = dc[l].astype(jnp.bfloat16)


def exchange_kernel(chips, groups, delta, cols, gate_hbm, cand_hbm, gate_out, cand_out, tok_out,
                    slots, weights, partial, landed, w_sem, own_sem, pass_sem, recv_sem, part_send, part_recv):
    seq = lax.axis_index("seq")
    tp = lax.axis_index("tp")
    chip = lax.div(seq, 2)
    core = lax.rem(seq, 2)
    sibling = chip * 2 + 1 - core
    block = weights.shape[2]
    mesh_id = pl.DeviceIdType.MESH

    last = chips - 1
    right = jnp.minimum(chip + 1, last) * 2 + core
    left = jnp.maximum(chip - 1, 0) * 2 + core
    barrier = pltpu.get_barrier_semaphore()

    @pl.when(chip < last)
    def _():
        pl.semaphore_signal(barrier, inc=1, device_id=(right, tp), device_id_type=mesh_id)

    @pl.when(chip > 0)
    def _():
        pl.semaphore_signal(barrier, inc=1, device_id=(left, tp), device_id_type=mesh_id)

    pl.semaphore_signal(barrier, inc=1, device_id=(sibling, tp), device_id_type=mesh_id)
    for d in range(1, groups):
        pl.semaphore_signal(barrier, inc=1, device_id=(seq, lax.rem(tp + d, groups)), device_id_type=mesh_id)

    def fetch(p, buf):
        rows = pl.ds(pl.multiple_of(lax.rem(tp + p, groups) * block, 128), block)
        return [
            pltpu.make_async_copy(w.at[rows, :], weights.at[buf, k], w_sem.at[buf, k])
            for k, w in enumerate((gate_hbm, cand_hbm))
        ]

    for copy in fetch(1 % groups, 0):
        copy.start()
    pl.semaphore_wait(barrier, groups + jnp.minimum(chip, 1) + jnp.minimum(last - chip, 1))

    def pass_on(kind, origin, target, way):
        return pltpu.make_async_remote_copy(
            src_ref=slots.at[origin, kind], dst_ref=slots.at[origin, kind], send_sem=pass_sem.at[way, origin, kind],
            recv_sem=recv_sem.at[origin, kind], device_id=(target, tp), device_id_type=mesh_id)

    def own(kind):
        return pltpu.make_async_copy(delta.at[kind], slots.at[seq, kind], own_sem.at[kind])

    for kind in range(2):
        own(kind).start()
    for kind in range(2):
        own(kind).wait()

        @pl.when(chip < last)
        def _():
            pass_on(kind, seq, right, 0).start()

        @pl.when(chip > 0)
        def _():
            pass_on(kind, seq, left, 1).start()

        pass_on(kind, seq, sibling, 2).start()

    nt = (((1,), (1,)), ((), ()))
    tn = (((0,), (0,)), ((), ()))
    f32 = jnp.float32

    def share(p, buf):
        for copy in fetch(p, buf):
            copy.wait()
        term = lax.dot_general(delta[0], weights[buf, 0], nt, preferred_element_type=f32)
        return term + lax.dot_general(delta[1], weights[buf, 1], nt, preferred_element_type=f32)

    def give(p):
        return pltpu.make_async_remote_copy(
            src_ref=partial.at[p - 1], dst_ref=landed.at[p - 1], send_sem=part_send.at[p - 1],
            recv_sem=part_recv.at[p - 1], device_id=(seq, lax.rem(tp + p, groups)), device_id_type=mesh_id)

    for p in range(1, groups):
        for copy in fetch((p + 1) % groups, p % 2):
            copy.start()
        partial[p - 1] = share(p, (p - 1) % 2).astype(jnp.bfloat16)
        give(p).start()
    mine = share(0, (groups - 1) % 2)
    for p in range(1, groups):
        give(p).wait()
        mine = mine + landed[p - 1].astype(f32)
    tok_out[...] = mine.astype(jnp.bfloat16)

    gate_out[...] = jnp.zeros_like(gate_out)
    cand_out[...] = jnp.zeros_like(cand_out)
    for kind, out in enumerate((gate_out, cand_out)):

        def take(origin):
            out[...] += lax.dot_general(cols[origin], slots[origin, kind], tn, preferred_element_type=f32)

        take(seq)
        pass_on(kind, sibling, sibling, 2).wait_recv()
        take(sibling)

        def step(e, carry):
            dist = lax.div(e, 2) + 1
            from_left = lax.rem(e, 2) == 0
            origin_chip = jnp.where(from_left, chip - dist, chip + dist)

            @pl.when((origin_chip >= 0) & (origin_chip <= last))
            def _():
                origin = origin_chip * 2 + core
                pass_on(kind, origin, sibling, 2).wait_recv()

                @pl.when(from_left & (chip < last))
                def _():
                    pass_on(kind, origin, right, 0).start()

                @pl.when(jnp.logical_not(from_left) & (chip > 0))
                def _():
                    pass_on(kind, origin, left, 1).start()

                pass_on(kind, origin, sibling, 2).start()
                take(origin)
                other = origin_chip * 2 + 1 - core
                pass_on(kind, other, sibling, 2).wait_recv()
                take(other)

            return carry

        lax.fori_loop(0, 2 * last, step, 0)
    for kind in range(2):

        def drain(o, carry):
            origin = o * 2 + core

            @pl.when((o <= chip) & (chip < last))
            def _():
                pass_on(kind, origin, right, 0).wait_send()

            @pl.when((o >= chip) & (chip > 0))
            def _():
                pass_on(kind, origin, left, 1).wait_send()

            pass_on(kind, origin, sibling, 2).wait_send()
            return carry

        lax.fori_loop(0, chips, drain, 0)


def shards(tokens, gate_weight, cand_weight, forget_bias, readout, advantage):
    devices = lax.axis_size("seq")
    groups = lax.axis_size("tp")
    whole = lax.all_gather(tokens, "tp", axis=2, tiled=True)
    count = whole.shape[1]
    depth = whole.shape[2]
    rows = 2 * count
    width = gate_weight.shape[1]
    flat = whole.reshape(rows, depth)
    part = rows // groups
    mine = lax.dynamic_slice_in_dim(flat, lax.axis_index("tp") * part, part, 0)
    mine = lax.all_to_all(mine, "seq", split_axis=1, concat_axis=0, tiled=True)
    cols = lax.all_gather(mine, "tp", axis=0, tiled=False)
    cols = cols.reshape(groups, devices, part, depth // devices)
    cols = jnp.transpose(cols, (1, 0, 2, 3)).reshape(devices, rows, depth // devices)

    scale = (advantage.astype(jnp.float32) * 0.25).reshape(rows, 1)
    read = readout.reshape(rows, width)
    tile = 256 if width % 256 == 0 else width
    f32 = jnp.float32
    col = pl.BlockSpec((rows, tile), lambda i: (0, i))
    lane = pl.BlockSpec((tile // LANE, rows, LANE), lambda i: (i, 0, 0))
    full_scale = pl.BlockSpec((rows, 1), lambda i: (0, 0))
    seg_spec = pl.BlockSpec((3, 2, SEGS, tile), lambda i: (0, 0, 0, i))
    keep, cand, seg, span = pl.pallas_call(
        project_kernel,
        grid=(width // tile,),
        in_specs=[
            pl.BlockSpec((rows, depth), lambda i: (0, 0)),
            pl.BlockSpec((depth, tile), lambda i: (0, i)),
            pl.BlockSpec((depth, tile), lambda i: (0, i)),
            pl.BlockSpec((1, tile), lambda i: (0, i)),
            col,
            full_scale,
        ],
        out_specs=[lane, lane, seg_spec, pl.BlockSpec((8, tile), lambda i: (0, i))],
        out_shape=[
            jax.ShapeDtypeStruct((width // LANE, rows, LANE), f32),
            jax.ShapeDtypeStruct((width // LANE, rows, LANE), f32),
            jax.ShapeDtypeStruct((3, 2, SEGS, width), f32),
            jax.ShapeDtypeStruct((8, width), f32),
        ],
        scratch_shapes=[pltpu.VMEM((tile // LANE, rows, LANE), f32)],
        compiler_params=pltpu.CompilerParams(vmem_limit_bytes=48 << 20),
        cost_estimate=pl.CostEstimate(flops=4 * rows * depth * width, bytes_accessed=4 * depth * width, transcendentals=rows * width),
    )(flat, gate_weight, cand_weight, forget_bias.reshape(1, width), read, scale)
    spans = lax.all_gather(span, "seq", axis=0, tiled=False)
    where = lax.axis_index("seq").astype(jnp.int32).reshape(1)
    delta = pl.pallas_call(
        functools.partial(delta_kernel, devices),
        grid=(width // tile,),
        in_specs=[
            pl.BlockSpec(memory_space=pltpu.SMEM),
            pl.BlockSpec((devices, 8, tile), lambda i: (0, 0, i)),
            seg_spec,
            lane,
            lane,
            col,
            full_scale,
        ],
        out_specs=pl.BlockSpec((2, rows, tile), lambda i: (0, 0, i)),
        out_shape=jax.ShapeDtypeStruct((2, rows, width), jnp.bfloat16),
        scratch_shapes=[pltpu.VMEM((tile // LANE, rows, LANE), f32)] * 3,
        compiler_params=pltpu.CompilerParams(vmem_limit_bytes=48 << 20),
    )(where, spans, seg, keep, cand, read, scale)

    chips = devices // 2
    block = depth // groups
    bf16 = jnp.bfloat16
    dma = pltpu.SemaphoreType.DMA
    vmem = pl.BlockSpec(memory_space=pltpu.VMEM)
    grad_gate, grad_cand, grad_tokens = pl.pallas_call(
        functools.partial(exchange_kernel, chips, groups),
        in_specs=[vmem, vmem, pl.BlockSpec(memory_space=pl.ANY), pl.BlockSpec(memory_space=pl.ANY)],
        out_specs=[vmem, vmem, vmem],
        out_shape=[
            jax.ShapeDtypeStruct((depth // devices, width), f32),
            jax.ShapeDtypeStruct((depth // devices, width), f32),
            jax.ShapeDtypeStruct((rows, block), bf16),
        ],
        scratch_shapes=[
            pltpu.VMEM((devices, 2, rows, width), bf16),
            pltpu.VMEM((2, 2, block, width), bf16),
            pltpu.VMEM((groups - 1, rows, block), bf16),
            pltpu.VMEM((groups - 1, rows, block), bf16),
            dma((2, 2)),
            dma((2,)),
            dma((3, devices, 2)),
            dma((devices, 2)),
            dma((groups - 1,)),
            dma((groups - 1,)),
        ],
        compiler_params=pltpu.CompilerParams(collective_id=1, has_side_effects=True, vmem_limit_bytes=56 << 20),
        cost_estimate=pl.CostEstimate(flops=12 * rows * depth * width, bytes_accessed=24 << 20, transcendentals=0),
    )(delta, cols, gate_weight, cand_weight)
    return (grad_gate, grad_cand, grad_tokens.reshape(2, count, block))


def solution(mesh):
    in_specs = (
        P(None, "seq", "tp"),
        P(None, "tp"),
        P(None, "tp"),
        P("tp"),
        P(None, "seq", "tp"),
        P(None, "seq"),
    )
    out_specs = (P("seq", "tp"), P("seq", "tp"), P(None, "seq", "tp"))
    return jax.shard_map(shards, mesh=mesh, in_specs=in_specs, out_specs=out_specs, check_vma=False)
```

```python
import functools

import jax
import jax.numpy as jnp
from jax import lax
from jax.experimental import pallas as pl
from jax.experimental.pallas import tpu as pltpu
from jax.sharding import PartitionSpec as P

SEGS = 8
LANE = 128


def front_kernel(devices, groups, tokens, gate_hbm, cand_hbm, bias, read, scale, delta_out, cols_out,
                 flat, weights, acc, keep, cand, score, dp, dc, seg, spans, cols,
                 w_sem, own_sem, tok_send, tok_recv, col_send, col_recv, span_send, span_recv):
    seq = lax.axis_index("seq")
    tp = lax.axis_index("tp")
    mesh_id = pl.DeviceIdType.MESH
    f32 = jnp.float32
    rows, block = tokens.shape
    count = rows // 2
    steps = count // SEGS
    lanes = keep.shape[0]
    part, deep = cols.shape[1:]
    per = devices // groups
    pack = 2 if lanes % 2 == 0 else 1

    barrier = pltpu.get_barrier_semaphore()
    for d in range(1, groups):
        pl.semaphore_signal(barrier, inc=1, device_id=(seq, lax.rem(tp + d, groups)), device_id_type=mesh_id)
    for d in range(1, devices):
        pl.semaphore_signal(barrier, inc=1, device_id=(lax.rem(seq + d, devices), tp), device_id_type=mesh_id)

    def fetch(p):
        at = pl.ds(pl.multiple_of(lax.rem(tp + p, groups) * block, 128), block)
        return [
            pltpu.make_async_copy(w.at[at, :], weights.at[k, p], w_sem.at[k, p])
            for k, w in enumerate((gate_hbm, cand_hbm))
        ]

    for p in range(groups):
        for copy in fetch(p):
            copy.start()
    own = pltpu.make_async_copy(tokens, flat.at[tp], own_sem.at[0])
    own.start()
    pl.semaphore_wait(barrier, groups - 1 + devices - 1)

    def tell(d):
        return pltpu.make_async_remote_copy(
            src_ref=tokens, dst_ref=flat.at[tp], send_sem=tok_send.at[d], recv_sem=tok_recv.at[tp],
            device_id=(seq, lax.rem(tp + d, groups)), device_id_type=mesh_id)

    def hear(source):
        return pltpu.make_async_remote_copy(
            src_ref=tokens, dst_ref=flat.at[source], send_sem=tok_send.at[0], recv_sem=tok_recv.at[source],
            device_id=(seq, lax.rem(tp + 1, groups)), device_id_type=mesh_id)

    for d in range(1, groups):
        tell(d).start()
    own.wait()

    def piece(source, r):
        return flat.at[source, pl.ds(pl.multiple_of(tp * part, 16), part), r * deep : (r + 1) * deep]

    def scatter(source, r):
        target = source * per + r
        return pltpu.make_async_remote_copy(
            src_ref=piece(source, r), dst_ref=cols.at[seq], send_sem=col_send.at[target],
            recv_sem=col_recv.at[seq], device_id=(target, tp), device_id_type=mesh_id)

    def gather(source):
        return pltpu.make_async_remote_copy(
            src_ref=cols.at[seq], dst_ref=cols.at[source], send_sem=col_send.at[source],
            recv_sem=col_recv.at[source], device_id=(lax.rem(seq + 1, devices), tp), device_id_type=mesh_id)

    def keep_piece(source, r):
        return pltpu.make_async_copy(piece(source, r), cols.at[seq], own_sem.at[1])

    for p in range(groups):
        source = lax.rem(tp + groups - p, groups)
        if p > 0:
            hear(source).wait_recv()
        for r in range(per):

            @pl.when(source * per + r != seq)
            def _():
                scatter(source, r).start()

            @pl.when(source * per + r == seq)
            def _():
                keep_piece(source, r).start()

        slot = (groups - p) % groups
        for k, copy in enumerate(fetch(slot)):
            copy.wait()
            term = jnp.dot(flat[source], weights[k, slot], preferred_element_type=f32)
            acc[k] = term if p == 0 else acc[k] + term

    def lane_of(l):
        return pl.ds(pl.multiple_of(l * LANE, LANE), LANE)

    def first(gi, carry):
        pairs = [(b, gi * pack + i) for b in range(2) for i in range(pack)]
        for i in range(pack):
            l = gi * pack + i
            at = lane_of(l)
            keep[l] = jax.nn.sigmoid(acc[0, :, at] + bias[:, at])
            cand[l] = acc[1, :, at]
            score[l] = scale[...] * read[:, at].astype(f32)
        zero = jnp.zeros((SEGS, LANE), f32)
        muls = [zero + 1.0 for _ in pairs]
        adds = [zero for _ in pairs]
        gs = [zero for _ in pairs]
        for i in range(steps):
            for p, (b, l) in enumerate(pairs):
                at = pl.ds(b * count + i, SEGS, stride=steps)
                k = keep[l, at, :]
                c = cand[l, at, :]
                muls[p] = muls[p] * k
                adds[p] = k * adds[p] + (1.0 - k) * c
                at = pl.ds(b * count + steps - 1 - i, SEGS, stride=steps)
                gs[p] = keep[l, at, :] * (score[l, at, :] + gs[p])
        for p, (b, l) in enumerate(pairs):
            mul, add, g = muls[p], adds[p], gs[p]
            seg[0, b, l] = mul
            seg[1, b, l] = add
            seg[2, b, l] = g
            m = mul[0:1]
            a = add[0:1]
            r = g[SEGS - 1 :]
            for j in range(1, SEGS):
                m = m * mul[j : j + 1]
                a = mul[j : j + 1] * a + add[j : j + 1]
                e = SEGS - 1 - j
                r = mul[e : e + 1] * r + g[e : e + 1]
            spans[seq, l, b : b + 1, :] = m
            spans[seq, l, 2 + b : 3 + b, :] = a
            spans[seq, l, 4 + b : 5 + b, :] = r
        for i in range(pack):
            spans[seq, gi * pack + i, 6:8, :] = jnp.zeros((2, LANE), f32)
        return carry

    lax.fori_loop(0, lanes // pack, first, 0)

    def span(d):
        return pltpu.make_async_remote_copy(
            src_ref=spans.at[seq], dst_ref=spans.at[seq], send_sem=span_send.at[d], recv_sem=span_recv.at[seq],
            device_id=(lax.rem(seq + d, devices), tp), device_id_type=mesh_id)

    def span_from(d):
        source = lax.rem(seq + d, devices)
        return pltpu.make_async_remote_copy(
            src_ref=spans.at[source], dst_ref=spans.at[source], send_sem=span_send.at[d],
            recv_sem=span_recv.at[source], device_id=(source, tp), device_id_type=mesh_id)

    for d in range(1, devices):
        span(d).start()
    for d in range(1, devices):
        span_from(d).wait_recv()

    def second(gi, carry):
        pairs = [(b, gi * pack + i) for b in range(2) for i in range(pack)]
        states, tails = [], []
        for b, l in pairs:
            a = jnp.zeros((1, LANE), f32)
            r = a
            for d in range(devices):
                e = devices - 1 - d
                a = jnp.where(d < seq, spans[d, l, b : b + 1, :] * a + spans[d, l, 2 + b : 3 + b, :], a)
                r = jnp.where(e > seq, spans[e, l, b : b + 1, :] * r + spans[e, l, 4 + b : 5 + b, :], r)
            mul, add, g = seg[0, b, l], seg[1, b, l], seg[2, b, l]
            starts, ends = [a], [r]
            for j in range(SEGS - 1):
                a = mul[j : j + 1] * a + add[j : j + 1]
                starts.append(a)
                e = SEGS - 1 - j
                r = mul[e : e + 1] * r + g[e : e + 1]
                ends.append(r)
            states.append(jnp.concatenate(starts, axis=0))
            tails.append(jnp.concatenate(ends[::-1], axis=0))
        for i in range(steps):
            for p, (b, l) in enumerate(pairs):
                at = pl.ds(b * count + i, SEGS, stride=steps)
                k = keep[l, at, :]
                c = cand[l, at, :]
                dp[l, at, :] = (states[p] - c) * k * (1.0 - k)
                states[p] = k * states[p] + (1.0 - k) * c
        for i in range(steps):
            for p, (b, l) in enumerate(pairs):
                at = pl.ds(b * count + steps - 1 - i, SEGS, stride=steps)
                k = keep[l, at, :]
                adj = score[l, at, :] + tails[p]
                dp[l, at, :] = adj * dp[l, at, :]
                dc[l, at, :] = adj * (1.0 - k)
                tails[p] = k * adj
        for i in range(pack):
            l = gi * pack + i
            delta_out[0, :, lane_of(l)] = dp[l].astype(jnp.bfloat16)
            delta_out[1, :, lane_of(l)] = dc[l].astype(jnp.bfloat16)
        return carry

    lax.fori_loop(0, lanes // pack, second, 0)

    for d in range(1, groups):
        tell(d).wait_send()
    for d in range(1, devices):
        span(d).wait_send()
    for p in range(groups):
        source = lax.rem(tp + groups - p, groups)
        for r in range(per):

            @pl.when(source * per + r != seq)
            def _():
                scatter(source, r).wait_send()

            @pl.when(source * per + r == seq)
            def _():
                keep_piece(source, r).wait()

    for d in range(1, devices):
        gather(lax.rem(seq + d, devices)).wait_recv()
    cols_out[...] = cols[...]


def exchange_kernel(chips, groups, delta, mine_cols, gate_hbm, cand_hbm, gate_out, cand_out, tok_out,
                    slots, cols, weights, partial, landed, w_sem, own_sem, pass_sem, recv_sem, part_send, part_recv, col_send, col_recv):
    seq = lax.axis_index("seq")
    tp = lax.axis_index("tp")
    chip = lax.div(seq, 2)
    core = lax.rem(seq, 2)
    sibling = chip * 2 + 1 - core
    block = weights.shape[2]
    mesh_id = pl.DeviceIdType.MESH

    last = chips - 1
    right = jnp.minimum(chip + 1, last) * 2 + core
    left = jnp.maximum(chip - 1, 0) * 2 + core
    barrier = pltpu.get_barrier_semaphore()

    @pl.when(chip < last)
    def _():
        pl.semaphore_signal(barrier, inc=1, device_id=(right, tp), device_id_type=mesh_id)

    @pl.when(chip > 0)
    def _():
        pl.semaphore_signal(barrier, inc=1, device_id=(left, tp), device_id_type=mesh_id)

    pl.semaphore_signal(barrier, inc=1, device_id=(sibling, tp), device_id_type=mesh_id)
    for d in range(1, groups):
        pl.semaphore_signal(barrier, inc=1, device_id=(seq, lax.rem(tp + d, groups)), device_id_type=mesh_id)

    def fetch(p, buf):
        rows = pl.ds(pl.multiple_of(lax.rem(tp + p, groups) * block, 128), block)
        return [
            pltpu.make_async_copy(w.at[rows, :], weights.at[buf, k], w_sem.at[buf, k])
            for k, w in enumerate((gate_hbm, cand_hbm))
        ]

    for copy in fetch(1 % groups, 0):
        copy.start()
    pl.semaphore_wait(barrier, groups + jnp.minimum(chip, 1) + jnp.minimum(last - chip, 1))

    def pass_on(kind, origin, target, way):
        return pltpu.make_async_remote_copy(
            src_ref=slots.at[origin, kind], dst_ref=slots.at[origin, kind], send_sem=pass_sem.at[way, origin, kind],
            recv_sem=recv_sem.at[origin, kind], device_id=(target, tp), device_id_type=mesh_id)

    def own(kind):
        return pltpu.make_async_copy(delta.at[kind], slots.at[seq, kind], own_sem.at[kind])

    for kind in range(2):
        own(kind).start()
    for kind in range(2):
        own(kind).wait()

        @pl.when(chip < last)
        def _():
            pass_on(kind, seq, right, 0).start()

        @pl.when(chip > 0)
        def _():
            pass_on(kind, seq, left, 1).start()

        pass_on(kind, seq, sibling, 2).start()

    def spread(d):
        return pltpu.make_async_remote_copy(
            src_ref=mine_cols, dst_ref=cols.at[tp], send_sem=col_send.at[d], recv_sem=col_recv.at[tp],
            device_id=(seq, lax.rem(tp + d, groups)), device_id_type=mesh_id)

    def spread_from(d):
        source = lax.rem(tp + d, groups)
        return pltpu.make_async_remote_copy(
            src_ref=mine_cols, dst_ref=cols.at[source], send_sem=col_send.at[d], recv_sem=col_recv.at[source],
            device_id=(seq, source), device_id_type=mesh_id)

    own_cols = pltpu.make_async_copy(mine_cols, cols.at[tp], own_sem.at[2])
    own_cols.start()
    for d in range(1, groups):
        spread(d).start()

    nt = (((1,), (1,)), ((), ()))
    tn = (((0,), (0,)), ((), ()))
    f32 = jnp.float32

    def share(p, buf):
        for copy in fetch(p, buf):
            copy.wait()
        term = lax.dot_general(delta[0], weights[buf, 0], nt, preferred_element_type=f32)
        return term + lax.dot_general(delta[1], weights[buf, 1], nt, preferred_element_type=f32)

    def give(p):
        return pltpu.make_async_remote_copy(
            src_ref=partial.at[p - 1], dst_ref=landed.at[p - 1], send_sem=part_send.at[p - 1],
            recv_sem=part_recv.at[p - 1], device_id=(seq, lax.rem(tp + p, groups)), device_id_type=mesh_id)

    for p in range(1, groups):
        for copy in fetch((p + 1) % groups, p % 2):
            copy.start()
        partial[p - 1] = share(p, (p - 1) % 2).astype(jnp.bfloat16)
        give(p).start()
    mine = share(0, (groups - 1) % 2)
    for p in range(1, groups):
        give(p).wait()
        mine = mine + landed[p - 1].astype(f32)
    tok_out[...] = mine.astype(jnp.bfloat16)

    own_cols.wait()
    for d in range(1, groups):
        spread(d).wait_send()
        spread_from(d).wait_recv()
    gate_out[...] = jnp.zeros_like(gate_out)
    cand_out[...] = jnp.zeros_like(cand_out)
    for kind, out in enumerate((gate_out, cand_out)):

        def take(origin):
            rows = jnp.concatenate([cols[g, origin] for g in range(groups)], axis=0)
            out[...] += lax.dot_general(rows, slots[origin, kind], tn, preferred_element_type=f32)

        take(seq)
        pass_on(kind, sibling, sibling, 2).wait_recv()
        take(sibling)

        def step(e, carry):
            dist = lax.div(e, 2) + 1
            from_left = lax.rem(e, 2) == 0
            origin_chip = jnp.where(from_left, chip - dist, chip + dist)

            @pl.when((origin_chip >= 0) & (origin_chip <= last))
            def _():
                origin = origin_chip * 2 + core
                pass_on(kind, origin, sibling, 2).wait_recv()

                @pl.when(from_left & (chip < last))
                def _():
                    pass_on(kind, origin, right, 0).start()

                @pl.when(jnp.logical_not(from_left) & (chip > 0))
                def _():
                    pass_on(kind, origin, left, 1).start()

                pass_on(kind, origin, sibling, 2).start()
                take(origin)
                other = origin_chip * 2 + 1 - core
                pass_on(kind, other, sibling, 2).wait_recv()
                take(other)

            return carry

        lax.fori_loop(0, 2 * last, step, 0)
    for kind in range(2):

        def drain(o, carry):
            origin = o * 2 + core

            @pl.when((o <= chip) & (chip < last))
            def _():
                pass_on(kind, origin, right, 0).wait_send()

            @pl.when((o >= chip) & (chip > 0))
            def _():
                pass_on(kind, origin, left, 1).wait_send()

            pass_on(kind, origin, sibling, 2).wait_send()
            return carry

        lax.fori_loop(0, chips, drain, 0)


def shards(tokens, gate_weight, cand_weight, forget_bias, readout, advantage):
    devices = lax.axis_size("seq")
    groups = lax.axis_size("tp")
    count = tokens.shape[1]
    rows = 2 * count
    depth, width = gate_weight.shape
    block = depth // groups
    part = rows // groups
    deep = depth // devices
    lanes = width // LANE
    f32 = jnp.float32
    bf16 = jnp.bfloat16
    dma = pltpu.SemaphoreType.DMA
    vmem = pl.BlockSpec(memory_space=pltpu.VMEM)
    hbm = pl.BlockSpec(memory_space=pl.ANY)
    scale = (advantage.astype(f32) * 0.25).reshape(rows, 1)
    plane = pltpu.VMEM((lanes, rows, LANE), f32)
    delta, cols = pl.pallas_call(
        functools.partial(front_kernel, devices, groups),
        in_specs=[vmem, hbm, hbm, vmem, vmem, vmem],
        out_specs=[vmem, vmem],
        out_shape=[
            jax.ShapeDtypeStruct((2, rows, width), bf16),
            jax.ShapeDtypeStruct((devices, part, deep), bf16),
        ],
        scratch_shapes=[
            pltpu.VMEM((groups, rows, block), bf16),
            pltpu.VMEM((2, groups, block, width), bf16),
            pltpu.VMEM((2, rows, width), f32),
            plane,
            plane,
            plane,
            plane,
            plane,
            pltpu.VMEM((3, 2, lanes, SEGS, LANE), f32),
            pltpu.VMEM((devices, lanes, 8, LANE), f32),
            pltpu.VMEM((devices, part, deep), bf16),
            dma((2, groups)),
            dma((2,)),
            dma((groups,)),
            dma((groups,)),
            dma((devices,)),
            dma((devices,)),
            dma((devices,)),
            dma((devices,)),
        ],
        compiler_params=pltpu.CompilerParams(collective_id=2, has_side_effects=True, vmem_limit_bytes=56 << 20),
        cost_estimate=pl.CostEstimate(flops=4 * rows * depth * width, bytes_accessed=20 << 20, transcendentals=rows * width),
    )(tokens.reshape(rows, block), gate_weight, cand_weight, forget_bias.reshape(1, width), readout.reshape(rows, width), scale)

    chips = devices // 2
    grad_gate, grad_cand, grad_tokens = pl.pallas_call(
        functools.partial(exchange_kernel, chips, groups),
        in_specs=[vmem, vmem, hbm, hbm],
        out_specs=[vmem, vmem, vmem],
        out_shape=[
            jax.ShapeDtypeStruct((depth // devices, width), f32),
            jax.ShapeDtypeStruct((depth // devices, width), f32),
            jax.ShapeDtypeStruct((rows, block), bf16),
        ],
        scratch_shapes=[
            pltpu.VMEM((devices, 2, rows, width), bf16),
            pltpu.VMEM((groups, devices, part, deep), bf16),
            pltpu.VMEM((2, 2, block, width), bf16),
            pltpu.VMEM((groups - 1, rows, block), bf16),
            pltpu.VMEM((groups - 1, rows, block), bf16),
            dma((2, 2)),
            dma((3,)),
            dma((3, devices, 2)),
            dma((devices, 2)),
            dma((groups - 1,)),
            dma((groups - 1,)),
            dma((groups,)),
            dma((groups,)),
        ],
        compiler_params=pltpu.CompilerParams(collective_id=1, has_side_effects=True, vmem_limit_bytes=56 << 20),
        cost_estimate=pl.CostEstimate(flops=12 * rows * depth * width, bytes_accessed=24 << 20, transcendentals=0),
    )(delta, cols, gate_weight, cand_weight)
    return (grad_gate, grad_cand, grad_tokens.reshape(2, count, block))


def solution(mesh):
    in_specs = (
        P(None, "seq", "tp"),
        P(None, "tp"),
        P(None, "tp"),
        P("tp"),
        P(None, "seq", "tp"),
        P(None, "seq"),
    )
    out_specs = (P("seq", "tp"), P("seq", "tp"), P(None, "seq", "tp"))
    return jax.shard_map(shards, mesh=mesh, in_specs=in_specs, out_specs=out_specs, check_vma=False)
```
